128 devices in a mesh: hst: 16 (over z, x), head: 8 (over y, core).
Axes of the slice: x: 4, y: 4, z: 4, core: 2. Of those that a mesh axis runs over, the one named last changes fastest.
Arguments:
- fresh_states: bfloat16 [8192, 8192], P('hst'), may hold values from -60 to 60
- query_states: bfloat16 [128, 8192], P('hst'), may hold values from -60 to 60
- w_query: bfloat16 [8192, 8192], P('hst', 'head'), may hold values from -0.0625 to 0.0625
- w_key: bfloat16 [8192, 1024], P('hst', 'head'), may hold values from -0.0625 to 0.0625
- w_value: bfloat16 [8192, 1024], P('hst', 'head'), may hold values from -0.0625 to 0.0625
- w_output: bfloat16 [8192, 8192], P('head', 'hst'), may hold values from -0.0625 to 0.0625
- cache_keys: bfloat16 [256, 256, 1024], P('hst', None, 'head'), may hold values from -6 to 6
- cache_values: bfloat16 [256, 256, 1024], P('hst', None, 'head'), may hold values from -6 to 6
- cached_mask: int32 [256], P('hst'), may hold values 0 or 1
- fresh_ids: int32 [32], P('hst'), may hold values from 0 to 255
- anchor_id: int32 [1], replicated, may hold values from 0 to 255
- query_pos: int32 [128], P('hst'), may hold values from 65536 to 65791
Outputs:
- fresh_context: bfloat16 [8192, 8192], P('hst', 'head')
- query_output: bfloat16 [128, 8192], P('head', 'hst')
The draws below stay inside these ranges and needn't reach their ends.
All inputs are finite; a program needn't handle non-finite values. No bound on the sum of `cached_mask` on one device may be relied on, other than what follows from the above.
Results may differ from the reference program's by a relative error of at most 0.039.
Values may be sent and summed in bfloat16 or wider, within the bound.
No kernel may reach another device: no remote copies, remote signals or barrier semaphores. Data moves between devices by JAX's collectives and lax.ppermute only.
A program may use at most 192 MiB of HBM per device.

```python
import math
import jax
import jax.numpy as jnp
from jax import lax

D = 8192
HQ = 64
KVH = 8
HD = 128
BLK = 256
BLK_DEV = 16
FRESH_BLK = 2
NBLK = 256
FRESH = 32
QROWS = 128
N_HST = 16


def draw_fresh_states(key, part):
    key = jax.random.fold_in(key, 11)
    base = jax.random.truncated_normal(key, -6.0, 6.0, (FRESH * BLK, D), jnp.float32)
    return base.astype(jnp.bfloat16)


def draw_query_states(key, part):
    key = jax.random.fold_in(key, 23)
    base = jax.random.truncated_normal(key, -6.0, 6.0, (QROWS, D), jnp.float32)
    return base.astype(jnp.bfloat16)


def place_ends(drawn, rng, low, top_value):
    longest = drawn.shape.index(max(drawn.shape))
    spots = []
    for shift in (0, 1):
        where = [jax.random.randint(jax.random.fold_in(rng, axis), (), 0, length) for axis, length in enumerate(drawn.shape)]
        where[longest] = (where[longest] + shift) % drawn.shape[longest]
        spots.append(tuple(where))
    return drawn.at[spots[0]].set(low).at[spots[1]].set(top_value)


def levels(own_key, shape, cuts, least, high):
    loudness, own = 1.0, jax.random.fold_in(own_key, 6)
    for dim, blocks in cuts:
        draws = jnp.exp(jax.random.uniform(jax.random.fold_in(own, dim), (blocks,), jnp.float32, least / len(cuts), high / len(cuts)))
        loudness = loudness * jnp.repeat(draws, shape[dim] // blocks).reshape([-1 if axis == dim else 1 for axis in range(len(shape))])
    return loudness


def bell_draw(key, extent, scale, reach, shards=(), kind=jnp.bfloat16):
    values = jax.random.normal(key, extent, jnp.float32) * scale
    if len(shards) > 0:
        values = levels(key, extent, shards, -0.22, 0.18) * values
    return jnp.clip(values, min=-reach, max=reach).astype(kind)


def setup_inputs(seed: int = 0) -> dict:
    streams_of = jax.random.split(jax.random.key(seed), 13)
    fresh_states = draw_fresh_states(jax.random.fold_in(streams_of[12], 71), 0)
    query_states = draw_query_states(jax.random.fold_in(streams_of[12], 71), 0)
    w_query = bell_draw(streams_of[2], (D, HQ * HD), D ** -0.5, 0.0625, ((0, 16), (1, 8)))
    w_key = bell_draw(streams_of[3], (D, KVH * HD), D ** -0.5, 0.0625, ((0, 16), (1, 8)))
    w_value = bell_draw(streams_of[4], (D, KVH * HD), D ** -0.5, 0.0625, ((0, 16), (1, 8)))
    w_output = bell_draw(streams_of[5], (HQ * HD, D), (HQ * HD) ** -0.5, 0.0625, ((0, 8), (1, 16)))
    cache_keys = bell_draw(streams_of[6], (NBLK, BLK, KVH * HD), 1.0, 6.0, ((0, 16), (2, 8)))
    cache_values = bell_draw(streams_of[7], (NBLK, BLK, KVH * HD), 1.0, 6.0, ((0, 16), (2, 8)))
    cached_mask = place_ends((jax.random.randint(streams_of[8], (NBLK,), 0, 4) < 3).astype(jnp.int32), jax.random.fold_in(streams_of[8], 1), 0, 1)
    fresh_ids = place_ends(jax.random.randint(streams_of[9], (FRESH,), 0, NBLK), jax.random.fold_in(streams_of[9], 1), 0, NBLK - 1).astype(jnp.int32)
    anchor_id = jax.random.randint(streams_of[10], (1,), 0, NBLK).astype(jnp.int32)
    query_pos = place_ends(jax.random.randint(streams_of[11], (QROWS,), NBLK * BLK, NBLK * BLK + BLK), jax.random.fold_in(streams_of[11], 1), NBLK * BLK, (NBLK * BLK + BLK) - 1).astype(jnp.int32)
    return dict(fresh_states=fresh_states, query_states=query_states, w_query=w_query, w_key=w_key, w_value=w_value, w_output=w_output, cache_keys=cache_keys, cache_values=cache_values, cached_mask=cached_mask, fresh_ids=fresh_ids, anchor_id=anchor_id, query_pos=query_pos)


ROPE_BASE = 500000.0

def scaled_rates(width):
    half = width // 2
    base_rates = ROPE_BASE ** (-jnp.arange(half, dtype=jnp.float32) * (2.0 / width))
    wavelength = 2.0 * math.pi / base_rates
    smooth = jnp.clip((8192.0 / wavelength - 1.0) / 3.0, 0.0, 1.0)
    return (1.0 - smooth) * base_rates / 8.0 + smooth * base_rates

def rotary(vectors, places):
    half = vectors.shape[-1] // 2
    rates = scaled_rates(vectors.shape[-1])
    angles = places.astype(jnp.float32)[:, None] * rates[None, :]
    cosine = jnp.cos(angles)[:, None, :]
    sine = jnp.sin(angles)[:, None, :]
    leading = vectors[..., :half]
    trailing = vectors[..., half:]
    return jnp.concatenate([leading * cosine - trailing * sine, trailing * cosine + leading * sine], axis=-1)

def reference(fresh_states, query_states, w_query, w_key, w_value, w_output, cache_keys, cache_values, cached_mask, fresh_ids, anchor_id, query_pos):
    per_group = HQ // KVH
    inverse_root = 1.0 / math.sqrt(HD)
    fresh_places = (fresh_ids[:, None] * BLK + jnp.arange(BLK, dtype=jnp.int32)[None, :]).reshape(-1).astype(jnp.int32)
    fresh_query = rotary(jnp.dot(fresh_states, w_query, preferred_element_type=jnp.float32).reshape(-1, HQ, HD), fresh_places).astype(jnp.bfloat16)
    fresh_key = rotary(jnp.dot(fresh_states, w_key, preferred_element_type=jnp.float32).reshape(-1, KVH, HD), fresh_places).astype(jnp.bfloat16)
    fresh_value = jnp.dot(fresh_states, w_value, preferred_element_type=jnp.float32).astype(jnp.bfloat16).reshape(-1, KVH, HD)
    query_heads = rotary(jnp.dot(query_states, w_query, preferred_element_type=jnp.float32).reshape(-1, HQ, HD), query_pos).astype(jnp.bfloat16)
    anchor = anchor_id[0].astype(jnp.int32)
    anchor_key = lax.dynamic_index_in_dim(cache_keys, anchor, 0, keepdims=False).reshape(BLK, KVH, HD).astype(jnp.float32)
    anchor_value = lax.dynamic_index_in_dim(cache_values, anchor, 0, keepdims=False).reshape(BLK, KVH, HD).astype(jnp.float32)
    causal = jnp.arange(BLK)[None, :] <= jnp.arange(BLK)[:, None]
    allowed = jnp.concatenate([jnp.ones((BLK, BLK), bool), causal], axis=1)

    def encode(pieces):
        block_query, block_key, block_value = pieces
        grouped = block_query.reshape(BLK, KVH, per_group, HD).astype(jnp.float32)
        keys_all = jnp.concatenate([anchor_key, block_key.astype(jnp.float32)], axis=0)
        values_all = jnp.concatenate([anchor_value, block_value.astype(jnp.float32)], axis=0)
        scores = jnp.einsum('qkgd,skd->kgqs', grouped, keys_all) * inverse_root
        scores = jnp.where(allowed, scores, -jnp.inf)
        highest = lax.optimization_barrier(jnp.max(scores, axis=-1, keepdims=True))
        raised = jnp.exp(scores - highest)
        probs = lax.optimization_barrier((raised / lax.optimization_barrier(jnp.sum(raised, axis=-1, keepdims=True))).astype(jnp.bfloat16))
        mixed = jnp.einsum('kgqs,skd->qkgd', probs.astype(jnp.float32), values_all)
        return mixed.astype(jnp.bfloat16).reshape(BLK, HQ * HD)
    fresh_context = lax.map(encode, (fresh_query.reshape(FRESH, BLK, HQ, HD), fresh_key.reshape(FRESH, BLK, KVH, HD), fresh_value.reshape(FRESH, BLK, KVH, HD)))
    fresh_context = fresh_context.reshape(FRESH * BLK, HQ * HD)
    query_grouped = query_heads.reshape(QROWS, KVH, per_group, HD).astype(jnp.float32)
    fresh_key_groups = fresh_key.reshape(N_HST, FRESH_BLK * BLK, KVH, HD)
    fresh_value_groups = fresh_value.reshape(N_HST, FRESH_BLK * BLK, KVH, HD)

    def attend(host):
        first_slot = (host * BLK_DEV).astype(jnp.int32)
        block_keys = lax.dynamic_slice_in_dim(cache_keys, first_slot, BLK_DEV, 0).reshape(BLK_DEV * BLK, KVH, HD)
        block_values = lax.dynamic_slice_in_dim(cache_values, first_slot, BLK_DEV, 0).reshape(BLK_DEV * BLK, KVH, HD)
        live_blocks = lax.dynamic_slice_in_dim(cached_mask, first_slot, BLK_DEV, 0)
        keys_all = jnp.concatenate([block_keys, lax.dynamic_index_in_dim(fresh_key_groups, host, 0, keepdims=False)], axis=0).astype(jnp.float32)
        values_all = jnp.concatenate([block_values, lax.dynamic_index_in_dim(fresh_value_groups, host, 0, keepdims=False)], axis=0).astype(jnp.float32)
        live = jnp.concatenate([jnp.repeat(live_blocks == 1, BLK), jnp.ones((FRESH_BLK * BLK,), bool)])
        scores = jnp.einsum('qkgd,skd->kgqs', query_grouped, keys_all) * inverse_root
        scores = jnp.where(live, scores, -jnp.inf)
        highest = lax.optimization_barrier(jnp.max(scores, axis=-1))
        raised = jnp.exp(scores - highest[..., None])
        totals = lax.optimization_barrier(jnp.sum(raised, axis=-1))
        rounded = lax.optimization_barrier(raised.astype(jnp.bfloat16))
        weighted = jnp.einsum('kgqs,skd->kgqd', rounded.astype(jnp.float32), values_all)
        return (highest, totals, weighted)
    peaks, totals, weighted = lax.map(attend, jnp.arange(N_HST, dtype=jnp.int32))
    top = lax.optimization_barrier(jnp.max(peaks, axis=0))
    factors = jnp.exp(peaks - top)
    total = lax.optimization_barrier(jnp.sum(totals * factors, axis=0))
    summed = lax.optimization_barrier(jnp.sum(weighted * factors[..., None], axis=0))
    query_context = (summed / total[..., None]).transpose(2, 0, 1, 3).reshape(QROWS, HQ * HD).astype(jnp.bfloat16)
    query_output = jnp.dot(query_context, w_output, preferred_element_type=jnp.float32).astype(jnp.bfloat16)
    return (fresh_context, query_output)
```

```python
import functools
import math

import jax
import jax.numpy as jnp
from jax import lax
from jax.experimental import pallas as pl
from jax.experimental.pallas import tpu as pltpu
from jax.sharding import PartitionSpec as P

HD = 128
BLK = 256
FRESH_BLK = 2
ROPE_BASE = 500000.0
N_HST = 16
N_HEAD = 8
SCALE = math.log2(math.e) / math.sqrt(HD)
BF16 = jnp.bfloat16
F32 = jnp.float32
VMEM_LIMIT = 48 * 1024 * 1024


def scaled_rates(width):
    half = width // 2
    base_rates = ROPE_BASE ** (-jnp.arange(half, dtype=F32) * (2.0 / width))
    wavelength = 2.0 * math.pi / base_rates
    smooth = jnp.clip((8192.0 / wavelength - 1.0) / 3.0, 0.0, 1.0)
    return (1.0 - smooth) * base_rates / 8.0 + smooth * base_rates


def rotary_tables(places):
    angles = places.astype(F32)[:, None] * scaled_rates(HD)[None, :]
    cosine, sine = jnp.cos(angles), jnp.sin(angles)
    return (
        jnp.concatenate([cosine, cosine], axis=1),
        jnp.concatenate([-sine, sine], axis=1),
    )


def rotate(vectors, cosine, sine):
    rows, cols = vectors.shape
    split = vectors.reshape(rows, cols // HD, HD)
    swapped = jnp.concatenate([split[..., HD // 2 :], split[..., : HD // 2]], axis=-1)
    return (split * cosine[:, None, :] + swapped * sine[:, None, :]).reshape(rows, cols)


def dot_t(a, b):
    return lax.dot_general(a, b, (((1,), (1,)), ((), ())), preferred_element_type=F32)


def fresh_kernel(q_ref, cos_ref, sin_ref, k_ref, v_ref, ak_ref, av_ref, out_ref):
    q = q_ref[...]
    q = (q * cos_ref[...] + pltpu.roll(q, HD // 2, 1) * sin_ref[...]).astype(BF16)
    row = lax.broadcasted_iota(jnp.int32, (BLK, BLK), 0)
    col = lax.broadcasted_iota(jnp.int32, (BLK, BLK), 1)
    causal = col <= row
    for b in range(FRESH_BLK):
        rows = slice(b * BLK, (b + 1) * BLK)
        qb = q[rows]
        s0 = dot_t(qb, ak_ref[...]) * SCALE
        s1 = jnp.where(causal, dot_t(qb, k_ref[rows, :]) * SCALE, -jnp.inf)
        top = jnp.max(jnp.maximum(s0, s1), axis=1, keepdims=True)
        e0 = jnp.exp2(s0 - top)
        e1 = jnp.exp2(s1 - top)
        total = jnp.sum(e0 + e1, axis=1, keepdims=True)
        mixed = jnp.dot(e0.astype(BF16), av_ref[...], preferred_element_type=F32)
        mixed += jnp.dot(e1.astype(BF16), v_ref[rows, :], preferred_element_type=F32)
        out_ref[rows, :] = (mixed / total).astype(BF16)


def fresh_attention(q, cosine, sine, key, value, anchor_key, anchor_value):
    rows, cols = q.shape
    whole = lambda a: pl.BlockSpec(a.shape, lambda i: (0, 0))
    return pl.pallas_call(
        fresh_kernel,
        grid=(cols // HD,),
        in_specs=[pl.BlockSpec((rows, HD), lambda i: (0, i))]
        + [whole(a) for a in (cosine, sine, key, value, anchor_key, anchor_value)],
        out_specs=pl.BlockSpec((rows, HD), lambda i: (0, i)),
        out_shape=jax.ShapeDtypeStruct((rows, cols), BF16),
        compiler_params=pltpu.CompilerParams(vmem_limit_bytes=VMEM_LIMIT),
        cost_estimate=pl.CostEstimate(
            flops=rows * (cols // HD) * 2 * BLK * HD * 4,
            bytes_accessed=rows * cols * 6,
            transcendentals=rows * (cols // HD) * 2 * BLK,
        ),
        name="fresh_attention",
    )(q, cosine, sine, key, value, anchor_key, anchor_value)


CHUNK = 512
STEP_HEADS = 2


def context_kernel(q_ref, ck_ref, cv_ref, fk_ref, fv_ref, bias_ref, out_ref, stat_ref, s_ref):
    step = pl.program_id(0)
    rows = q_ref.shape[0]
    q = jnp.concatenate([q_ref[:, g * HD : (g + 1) * HD] for g in range(STEP_HEADS)], axis=0)
    cached = ck_ref.shape[0]
    parts = [(ck_ref, cv_ref, i, i) for i in range(0, cached, CHUNK)]
    parts += [(fk_ref, fv_ref, i, cached + i) for i in range(0, fk_ref.shape[0], CHUNK)]
    top = None
    for keys, _, at, place in parts:
        s = dot_t(q, keys[at : at + CHUNK, :]) * SCALE
        if keys is ck_ref:
            s = s + bias_ref[:, place : place + CHUNK]
        s_ref[:, place : place + CHUNK] = s
        for j in range(0, CHUNK, HD):
            top = s[:, j : j + HD] if top is None else jnp.maximum(top, s[:, j : j + HD])
    peak = jnp.max(top, axis=1, keepdims=True)
    total = jnp.zeros((q.shape[0], HD), F32)
    acc = jnp.zeros((q.shape[0], HD), F32)
    for _, values, at, place in parts:
        e = jnp.exp2(s_ref[:, place : place + CHUNK] - peak)
        for j in range(0, CHUNK, HD):
            total += e[:, j : j + HD]
        acc += jnp.dot(e.astype(BF16), values[at : at + CHUNK, :], preferred_element_type=F32)
    total = jnp.sum(total, axis=1, keepdims=True)

    @pl.when(step == 0)
    def _():
        stat_ref[...] = jnp.zeros_like(stat_ref)

    lane = lax.broadcasted_iota(jnp.int32, (rows, HD), 1)
    stats = stat_ref[...]
    for g in range(STEP_HEADS):
        block = slice(g * rows, (g + 1) * rows)
        out_ref[:, g * HD : (g + 1) * HD] = acc[block]
        head = step * STEP_HEADS + g
        stats = jnp.where(lane == head, peak[block], stats)
        stats = jnp.where(lane == head + N_HEAD, total[block], stats)
    stat_ref[...] = stats


def context_attention(q, cache_key, cache_value, key, value, bias):
    rows, cols = q.shape
    heads = cols // HD
    wide = STEP_HEADS * HD
    keys = cache_key.shape[0] + key.shape[0]
    whole = lambda a: pl.BlockSpec(a.shape, lambda i: (0, 0))
    return pl.pallas_call(
        context_kernel,
        grid=(heads // STEP_HEADS,),
        in_specs=[pl.BlockSpec((rows, wide), lambda i: (0, i))]
        + [whole(a) for a in (cache_key, cache_value, key, value, bias)],
        out_specs=[
            pl.BlockSpec((rows, wide), lambda i: (0, i)),
            pl.BlockSpec((rows, HD), lambda i: (0, 0)),
        ],
        out_shape=[
            jax.ShapeDtypeStruct((rows, cols), F32),
            jax.ShapeDtypeStruct((rows, HD), F32),
        ],
        scratch_shapes=[pltpu.VMEM((STEP_HEADS * rows, keys), F32)],
        compiler_params=pltpu.CompilerParams(vmem_limit_bytes=VMEM_LIMIT),
        cost_estimate=pl.CostEstimate(
            flops=rows * heads * keys * HD * 4,
            bytes_accessed=keys * HD * 4 + rows * cols * 6,
            transcendentals=rows * heads * keys,
        ),
        name="context_attention",
    )(q, cache_key, cache_value, key, value, bias)


def exchange(value, axis):
    return lax.all_to_all(value, axis, 0, 0, tiled=True)


def spread(value, axis, count):
    return exchange(jnp.broadcast_to(value[None], (count,) + value.shape), axis)


def body(
    fresh_states,
    query_states,
    w_query,
    w_key,
    w_value,
    w_output,
    cache_keys,
    cache_values,
    cached_mask,
    fresh_ids,
    anchor_id,
    query_pos,
):
    fresh_rows = fresh_states.shape[0]
    query_rows, width = query_states.shape
    depth, query_cols = w_query.shape
    held_blocks = cache_keys.shape[0]

    w_both = lax.all_gather(
        jnp.concatenate([w_key, w_value], axis=1), "hst", axis=0, tiled=True
    )
    w_query_all = lax.all_gather(w_query, "hst", axis=0, tiled=True)

    anchor = anchor_id[0]
    mine = lax.axis_index("hst") == anchor // held_blocks
    slot = anchor % held_blocks
    anchor_parts = [
        jnp.where(mine, lax.dynamic_index_in_dim(a, slot, 0, keepdims=False), 0).reshape(
            N_HST, -1, depth
        )
        for a in (cache_keys, cache_values)
    ]
    states = query_states.reshape(query_rows, N_HST, depth).transpose(1, 0, 2)
    got = exchange(jnp.concatenate([states] + anchor_parts, axis=1), "hst")
    own_anchor = jnp.sum(got[:, query_rows:].astype(F32), axis=0).astype(BF16)
    states = got[:, :query_rows].reshape(N_HST * query_rows, depth)

    partial = jnp.dot(states, w_query, preferred_element_type=F32).astype(BF16)
    partial = exchange(partial.reshape(N_HST, query_rows, query_cols), "hst")
    query_cos, query_sin = rotary_tables(query_pos)
    own_queries = rotate(jnp.sum(partial.astype(F32), axis=0), query_cos, query_sin).astype(BF16)
    packed = jnp.concatenate([own_queries, own_anchor.reshape(-1, query_cols)], axis=0)
    packed = spread(packed, "hst", N_HST)
    all_queries = packed[:, :query_rows].reshape(N_HST * query_rows, query_cols)
    anchors = packed[:, query_rows:].reshape(N_HST, 2, BLK // N_HST, HD)
    anchor_key = anchors[:, 0].reshape(BLK, HD)
    anchor_value = anchors[:, 1].reshape(BLK, HD)

    places = (fresh_ids[:, None] * BLK + jnp.arange(BLK, dtype=jnp.int32)[None, :]).reshape(-1)
    cosine, sine = rotary_tables(places)
    both = jnp.dot(fresh_states, w_both, preferred_element_type=F32)
    fresh_key = rotate(both[:, :HD], cosine, sine).astype(BF16)
    fresh_value = both[:, HD:].astype(BF16)

    live = jnp.repeat(cached_mask == 1, BLK)
    bias = jnp.where(live, 0.0, -jnp.inf).astype(F32)[None, :]
    weighted, stats = context_attention(
        all_queries,
        cache_keys.reshape(-1, HD),
        cache_values.reshape(-1, HD),
        fresh_key,
        fresh_value,
        bias,
    )
    sums = exchange(
        jnp.concatenate([weighted, stats], axis=1).reshape(N_HST, query_rows, -1), "hst"
    )
    weighted = sums[..., :query_cols].reshape(N_HST, query_rows, N_HEAD, HD)
    peaks = sums[..., query_cols : query_cols + N_HEAD]
    totals = sums[..., query_cols + N_HEAD : query_cols + 2 * N_HEAD]
    factors = jnp.exp2(peaks - jnp.max(peaks, axis=0))
    total = jnp.sum(totals * factors, axis=0)
    context = jnp.sum(weighted * factors[..., None], axis=0) / total[..., None]
    context = spread(context.reshape(query_rows, query_cols).astype(BF16), "hst", N_HST)
    product = jnp.dot(
        context.reshape(N_HST * query_rows, query_cols), w_output, preferred_element_type=F32
    )
    product = exchange(product.reshape(N_HEAD, -1, product.shape[1]), "head")
    query_output = jnp.sum(product, axis=0).astype(BF16)

    query = jnp.dot(fresh_states, w_query_all, preferred_element_type=F32)
    fresh_context = fresh_attention(
        query, cosine, sine, fresh_key, fresh_value, anchor_key, anchor_value
    )
    return fresh_context, query_output


def solution(mesh):
    return jax.shard_map(
        body,
        mesh=mesh,
        in_specs=(
            P("hst", None),
            P("hst", None),
            P("hst", "head"),
            P("hst", "head"),
            P("hst", "head"),
            P("head", "hst"),
            P("hst", None, "head"),
            P("hst", None, "head"),
            P("hst"),
            P("hst"),
            P(),
            P("hst"),
        ),
        out_specs=(P("hst", "head"), P("head", "hst")),
        check_vma=False,
    )
```

```python
import functools
import math

import jax
import jax.numpy as jnp
from jax import lax
from jax.experimental import pallas as pl
from jax.experimental.pallas import tpu as pltpu
from jax.sharding import Mesh
from jax.sharding import PartitionSpec as P

HD = 128
BLK = 256
FRESH_BLK = 2
ROPE_BASE = 500000.0
N_HST = 16
N_HEAD = 8
RING = 4
STEP_HEADS = 2
HST = ("z", "x")
HEAD = ("y", "core")
SCALE = math.log2(math.e) / math.sqrt(HD)
BF16 = jnp.bfloat16
F32 = jnp.float32
VMEM_LIMIT = 48 * 1024 * 1024
DEAD = -1e30


def scaled_rates(width):
    half = width // 2
    base_rates = ROPE_BASE ** (-jnp.arange(half, dtype=F32) * (2.0 / width))
    wavelength = 2.0 * math.pi / base_rates
    smooth = jnp.clip((8192.0 / wavelength - 1.0) / 3.0, 0.0, 1.0)
    return (1.0 - smooth) * base_rates / 8.0 + smooth * base_rates


def rotary_tables(places):
    angles = places.astype(F32)[:, None] * scaled_rates(HD)[None, :]
    cosine, sine = jnp.cos(angles), jnp.sin(angles)
    return (
        jnp.concatenate([cosine, cosine], axis=1),
        jnp.concatenate([-sine, sine], axis=1),
    )


def rotate(vectors, cosine, sine):
    rows, cols = vectors.shape
    split = vectors.reshape(rows, cols // HD, HD)
    swapped = jnp.concatenate([split[..., HD // 2 :], split[..., : HD // 2]], axis=-1)
    return (split * cosine[:, None, :] + swapped * sine[:, None, :]).reshape(rows, cols)


def dot_t(a, b):
    return lax.dot_general(a, b, (((1,), (1,)), ((), ())), preferred_element_type=F32)


def fresh_kernel(count, *refs):
    parts, refs = refs[:count], refs[count:]
    cos_ref, sin_ref, k_ref, v_ref, ak_ref, av_ref, out_ref = refs
    row = lax.broadcasted_iota(jnp.int32, (BLK, BLK), 0)
    col = lax.broadcasted_iota(jnp.int32, (BLK, BLK), 1)
    causal = col <= row
    for g in range(out_ref.shape[1] // HD):
        cols = slice(g * HD, (g + 1) * HD)
        q = parts[0][:, cols].astype(F32)
        for part in parts[1:]:
            q += part[:, cols].astype(F32)
        q = (q * cos_ref[...] + pltpu.roll(q, HD // 2, 1) * sin_ref[...]).astype(BF16)
        for b in range(FRESH_BLK):
            rows = slice(b * BLK, (b + 1) * BLK)
            qb = q[rows]
            s0 = dot_t(qb, ak_ref[...]) * SCALE
            s1 = jnp.where(causal, dot_t(qb, k_ref[rows, :]) * SCALE, -jnp.inf)
            top = jnp.max(jnp.maximum(s0, s1), axis=1, keepdims=True)
            e0 = jnp.exp2(s0 - top)
            e1 = jnp.exp2(s1 - top)
            total = jnp.sum(e0 + e1, axis=1, keepdims=True)
            mixed = jnp.dot(e0.astype(BF16), av_ref[...], preferred_element_type=F32)
            mixed += jnp.dot(e1.astype(BF16), v_ref[rows, :], preferred_element_type=F32)
            out_ref[rows, cols] = (mixed / total).astype(BF16)


def fresh_attention(parts, rest):
    rows, cols = parts[0].shape
    wide = STEP_HEADS * HD
    whole = lambda a: pl.BlockSpec(a.shape, lambda i: (0, 0))
    return pl.pallas_call(
        functools.partial(fresh_kernel, len(parts)),
        grid=(cols // wide,),
        in_specs=[pl.BlockSpec((rows, wide), lambda i: (0, i))] * len(parts)
        + [whole(a) for a in rest],
        out_specs=pl.BlockSpec((rows, wide), lambda i: (0, i)),
        out_shape=jax.ShapeDtypeStruct((rows, cols), BF16),
        compiler_params=pltpu.CompilerParams(vmem_limit_bytes=VMEM_LIMIT),
        cost_estimate=pl.CostEstimate(
            flops=rows * (cols // HD) * 2 * BLK * HD * 4,
            bytes_accessed=rows * cols * 4,
            transcendentals=rows * (cols // HD) * 2 * BLK,
        ),
        name="fresh_attention",
    )(*parts, *rest)


def shares_kernel(count, place_ref, states_ref, *refs):
    pieces, w_refs = refs[:count], refs[count : count + 5]
    out_ref, t_v, w_v, o_v, t_sem, s_sem, w_sem, o_sem = refs[count + 5 :]
    blocks, rows, depth = t_v.shape
    slab = pieces[0].shape[1]
    own_copy = pltpu.make_async_copy(
        states_ref.at[:, pl.ds(pl.multiple_of(place_ref[0] * depth, depth), depth)],
        t_v.at[0],
        s_sem,
    )
    own_copy.start()
    w_copies = []
    for i, ref in enumerate(w_refs):
        at = pl.multiple_of(place_ref[blocks + count + i], slab)
        copy = pltpu.make_async_copy(ref, w_v.at[pl.ds(at, ref.shape[0]), :], w_sem.at[i])
        copy.start()
        w_copies.append(copy)
    copies = []
    for b in range(blocks - 1):
        for i, piece in enumerate(pieces):
            copy = pltpu.make_async_copy(
                piece.at[pl.ds(b * rows, rows), :],
                t_v.at[b + 1, :, pl.ds(pl.multiple_of(place_ref[blocks + i], slab), slab)],
                t_sem.at[b, i],
            )
            copy.start()
            copies.append(copy)
    own_copy.wait()
    for copy in w_copies:
        copy.wait()
    out_copies = []
    for b in range(blocks):
        if b > 0:
            for copy in copies[(b - 1) * count : b * count]:
                copy.wait()
        for n in range(0, w_v.shape[1], COLS):
            o_v[b, :, n : n + COLS] = jnp.dot(
                t_v[b], w_v[:, n : n + COLS], preferred_element_type=F32
            ).astype(BF16)
        copy = pltpu.make_async_copy(o_v.at[b], out_ref.at[place_ref[b]], o_sem.at[b])
        copy.start()
        out_copies.append(copy)
    for copy in out_copies:
        copy.wait()


def share_products(places, states, pieces, weights):
    blocks = RING
    rows = states.shape[0]
    depth = blocks * weights[0].shape[0]
    cols = weights[0].shape[1]
    anywhere = pl.BlockSpec(memory_space=pl.ANY)
    return pl.pallas_call(
        functools.partial(shares_kernel, len(pieces)),
        grid_spec=pltpu.PrefetchScalarGridSpec(
            num_scalar_prefetch=1,
            grid=(1,),
            in_specs=[anywhere] * (1 + len(pieces) + len(weights)),
            out_specs=anywhere,
            scratch_shapes=[
                pltpu.VMEM((blocks, rows, depth), BF16),
                pltpu.VMEM((depth, cols), BF16),
                pltpu.VMEM((blocks, rows, cols), BF16),
                pltpu.SemaphoreType.DMA((blocks - 1, len(pieces))),
                pltpu.SemaphoreType.DMA,
                pltpu.SemaphoreType.DMA((len(weights),)),
                pltpu.SemaphoreType.DMA((blocks,)),
            ],
        ),
        out_shape=jax.ShapeDtypeStruct((blocks, rows, cols), BF16),
        compiler_params=pltpu.CompilerParams(vmem_limit_bytes=VMEM_LIMIT),
        cost_estimate=pl.CostEstimate(
            flops=blocks * rows * depth * cols * 2,
            bytes_accessed=(blocks * rows * (depth + cols) + depth * cols) * 2,
            transcendentals=0,
        ),
        name="share_products",
    )(places, states, *pieces, *weights)


def key_value_kernel(states_ref, w_ref, cos_ref, sin_ref, k_ref, v_ref, acc_ref):
    step = pl.program_id(0)

    @pl.when(step == 0)
    def _():
        acc_ref[...] = jnp.zeros_like(acc_ref)

    acc_ref[...] += jnp.dot(states_ref[...], w_ref[...], preferred_element_type=F32)

    @pl.when(step == pl.num_programs(0) - 1)
    def _():
        k = acc_ref[:, :HD]
        k = k * cos_ref[...] + pltpu.roll(k, HD // 2, 1) * sin_ref[...]
        k_ref[...] = k.astype(BF16)
        v_ref[...] = acc_ref[:, HD:].astype(BF16)


def key_value(states, weights, cosine, sine):
    rows, depth = states.shape
    step = 1024
    whole = lambda a: pl.BlockSpec(a.shape, lambda i: (0, 0))
    out = jax.ShapeDtypeStruct((rows, HD), BF16)
    return pl.pallas_call(
        key_value_kernel,
        grid=(depth // step,),
        in_specs=[
            pl.BlockSpec((rows, step), lambda i: (0, i)),
            pl.BlockSpec((step, 2 * HD), lambda i: (i, 0)),
            whole(cosine),
            whole(sine),
        ],
        out_specs=[whole(out), whole(out)],
        out_shape=[out, out],
        scratch_shapes=[pltpu.VMEM((rows, 2 * HD), F32)],
        compiler_params=pltpu.CompilerParams(vmem_limit_bytes=VMEM_LIMIT),
        cost_estimate=pl.CostEstimate(
            flops=rows * depth * 4 * HD,
            bytes_accessed=(rows + 2 * HD) * depth * 2,
            transcendentals=0,
        ),
        name="key_value",
    )(states, weights, cosine, sine)


CHUNK = 512
COLS = 512


def pieces_of(value):
    high = value.astype(BF16).astype(F32)
    middle = (value - high).astype(BF16).astype(F32)
    return high, middle, value - high - middle


def cached_kernel(q_ref, k_ref, v_ref, bias_ref, out_ref, stat_ref, s_ref):
    step = pl.program_id(0)
    rows = q_ref.shape[0]
    q = jnp.concatenate([q_ref[:, g * HD : (g + 1) * HD] for g in range(STEP_HEADS)], axis=0)
    places = range(0, k_ref.shape[0], CHUNK)
    top = None
    for at in places:
        s = dot_t(q, k_ref[at : at + CHUNK, :]) * SCALE + bias_ref[:, at : at + CHUNK]
        s_ref[:, at : at + CHUNK] = s
        for j in range(0, CHUNK, HD):
            top = s[:, j : j + HD] if top is None else jnp.maximum(top, s[:, j : j + HD])
    peak = jnp.max(top, axis=1, keepdims=True)
    total = jnp.zeros((q.shape[0], HD), F32)
    acc = jnp.zeros((q.shape[0], HD), F32)
    for at in places:
        e = jnp.exp2(s_ref[:, at : at + CHUNK] - peak)
        for j in range(0, CHUNK, HD):
            total += e[:, j : j + HD]
        acc += jnp.dot(e.astype(BF16), v_ref[at : at + CHUNK, :], preferred_element_type=F32)
    total = jnp.sum(total, axis=1, keepdims=True)

    @pl.when(step == 0)
    def _():
        stat_ref[...] = jnp.zeros_like(stat_ref)

    lane = lax.broadcasted_iota(jnp.int32, (rows, HD), 1)
    stats = stat_ref[...]
    for g in range(STEP_HEADS):
        block = slice(g * rows, (g + 1) * rows)
        for n, number in enumerate((peak, total)):
            place = step * STEP_HEADS + g + n * N_HEAD
            stats = jnp.where(lane == place, number[block], stats)
        out_ref[:, g * HD : (g + 1) * HD] = acc[block]
    stat_ref[...] = stats


def cached_attention(q, key, value, bias):
    rows, cols = q.shape
    wide = STEP_HEADS * HD
    keys = key.shape[0]
    whole = lambda a: pl.BlockSpec(a.shape, lambda i: (0, 0))
    stats = jax.ShapeDtypeStruct((rows, HD), F32)
    return pl.pallas_call(
        cached_kernel,
        grid=(cols // wide,),
        in_specs=[pl.BlockSpec((rows, wide), lambda i: (0, i))]
        + [whole(a) for a in (key, value, bias)],
        out_specs=[pl.BlockSpec((rows, wide), lambda i: (0, i)), whole(stats)],
        out_shape=[jax.ShapeDtypeStruct((rows, cols), F32), stats],
        scratch_shapes=[pltpu.VMEM((STEP_HEADS * rows, keys), F32)],
        compiler_params=pltpu.CompilerParams(vmem_limit_bytes=VMEM_LIMIT),
        cost_estimate=pl.CostEstimate(
            flops=rows * cols * keys * 4,
            bytes_accessed=keys * HD * 4 + rows * cols * 4,
            transcendentals=rows * (cols // HD) * keys,
        ),
        name="cached_attention",
    )(q, key, value, bias)


def context_kernel(q_ref, k_ref, v_ref, old_ref, stat_ref, out_ref):
    rows, cols = q_ref.shape
    heads = cols // HD
    lane = lax.broadcasted_iota(jnp.int32, (rows, HD), 1)
    old_stats = stat_ref[...]
    stats = jnp.zeros((rows, HD), F32)
    for first in range(0, heads, STEP_HEADS):
        group = range(first, first + STEP_HEADS)
        q = jnp.concatenate([q_ref[:, g * HD : (g + 1) * HD] for g in group], axis=0)
        old = jnp.concatenate([old_ref[:, g * HD : (g + 1) * HD] for g in group], axis=0)
        old_peak = jnp.concatenate([old_stats[:, g : g + 1] for g in group], axis=0)
        old_total = jnp.concatenate(
            [old_stats[:, N_HEAD + g : N_HEAD + g + 1] for g in group], axis=0
        )
        s = dot_t(q, k_ref[...]) * SCALE
        peak = jnp.maximum(jnp.max(s, axis=1, keepdims=True), old_peak)
        e = jnp.exp2(s - peak)
        factor = jnp.exp2(old_peak - peak)
        total = jnp.sum(e, axis=1, keepdims=True) + old_total * factor
        acc = jnp.dot(e.astype(BF16), v_ref[...], preferred_element_type=F32) + old * factor
        numbers = pieces_of(peak) + pieces_of(total)
        for i, g in enumerate(group):
            block = slice(i * rows, (i + 1) * rows)
            for n, number in enumerate(numbers):
                stats = jnp.where(lane == g + n * N_HEAD, number[block], stats)
            out_ref[:, g * HD : (g + 1) * HD] = acc[block].astype(BF16)
    out_ref[:, cols:] = stats.astype(BF16)


def context_attention(q, key, value, old, old_stats):
    rows, cols = q.shape
    keys = key.shape[0]
    return pl.pallas_call(
        context_kernel,
        out_shape=jax.ShapeDtypeStruct((rows, cols + HD), BF16),
        compiler_params=pltpu.CompilerParams(vmem_limit_bytes=VMEM_LIMIT),
        cost_estimate=pl.CostEstimate(
            flops=rows * cols * keys * 4,
            bytes_accessed=keys * HD * 4 + rows * cols * 8,
            transcendentals=rows * (cols // HD) * keys,
        ),
        name="context_attention",
    )(q, key, value, old, old_stats)


def combine_kernel(parts_ref, out_ref):
    heads = out_ref.shape[2] // HD
    stats = parts_ref[:, :, heads * HD :].astype(F32)
    stats = (
        stats
        + pltpu.roll(stats, HD - N_HEAD, 2)
        + pltpu.roll(stats, HD - 2 * N_HEAD, 2)
    )
    factors = jnp.exp2(stats - jnp.max(stats, axis=0, keepdims=True))
    totals = pltpu.roll(stats, HD - 3 * N_HEAD, 2)
    share = factors / jnp.sum(totals * factors, axis=0, keepdims=True)
    for g in range(heads):
        cols = slice(g * HD, (g + 1) * HD)
        mixed = jnp.sum(parts_ref[:, :, cols].astype(F32) * share[:, :, g : g + 1], axis=0)
        out_ref[:, :, cols] = jnp.broadcast_to(
            mixed.astype(BF16)[None], out_ref.shape[:2] + (HD,)
        )


def combine(parts):
    groups, rows, cols = parts.shape
    return pl.pallas_call(
        combine_kernel,
        out_shape=jax.ShapeDtypeStruct((groups, rows, cols - HD), BF16),
        compiler_params=pltpu.CompilerParams(vmem_limit_bytes=VMEM_LIMIT),
        name="combine",
    )(parts)


def shift(value, axis, by):
    size = RING if axis != "core" else 2
    return lax.ppermute(value, axis, [(i, (i + by) % size) for i in range(size)])


def exchange(value, axis):
    return lax.all_to_all(value, axis, 0, 0, tiled=True)


def spread(value, axis, count):
    return exchange(jnp.broadcast_to(value[None], (count,) + value.shape), axis)


def body(
    fresh_states,
    query_states,
    w_query,
    w_key,
    w_value,
    w_output,
    cache_keys,
    cache_values,
    cached_mask,
    fresh_ids,
    anchor_id,
    query_pos,
):
    fresh_rows = fresh_states.shape[0]
    query_rows, width = query_states.shape
    depth, query_cols = w_query.shape
    held_blocks = cache_keys.shape[0]

    w_both = lax.all_gather(
        jnp.concatenate([w_key, w_value], axis=1), HST, axis=0, tiled=True
    )

    z, x, y, core = (lax.axis_index(a) for a in ("z", "x", "y", "core"))
    quarter = width // RING
    slab = quarter // N_HEAD
    steps = (1, -1, 2)
    slices = [
        lax.dynamic_slice_in_dim(
            fresh_states,
            lax.rem(z + d + RING, RING) * quarter + (y * 2 + core) * slab,
            slab,
            axis=1,
        )
        for d in steps
    ]
    owners = lax.rem(y + jnp.arange(RING, dtype=jnp.int32), RING) * 2
    at = jnp.concatenate([owners + core, owners + 1 - core]) * slab
    sources = jnp.stack([lax.rem(z - d + RING, RING) for d in steps])
    behind, ahead = shift(w_query, "x", 1), shift(w_query, "x", -1)
    middle = depth // 2
    turn = lax.rem(x + jnp.array([0, 1, 3, 2, 2], jnp.int32), RING) * depth
    turn = turn + jnp.array([0, 0, 0, 0, middle], jnp.int32)
    spots = jnp.concatenate([z[None], sources, at, turn])

    anchor = anchor_id[0]
    holder = lax.axis_index(HST) == anchor // held_blocks
    held = anchor % held_blocks
    anchor_parts = [
        jnp.where(holder, lax.dynamic_index_in_dim(a, held, 0, keepdims=False), 0).reshape(
            N_HST, -1, depth
        )
        for a in (cache_keys, cache_values)
    ]
    states = query_states.reshape(query_rows, N_HST, depth).transpose(1, 0, 2)
    packed = jnp.concatenate([states] + anchor_parts, axis=1)
    packed, slices = lax.optimization_barrier((packed, slices))
    mine = jnp.concatenate([shift(v, "z", d) for v, d in zip(slices, steps)], axis=0)
    got = exchange(packed, HST)
    got, mine = lax.optimization_barrier((got, mine))
    pieces = [mine, shift(mine, "y", -1), shift(mine, "y", 2), shift(mine, "y", 1)]
    own_anchor = jnp.sum(got[:, query_rows:].astype(F32), axis=0).astype(BF16)
    states = got[:, :query_rows].reshape(N_HST * query_rows, depth)

    partial = jnp.dot(states, w_query, preferred_element_type=F32).astype(BF16)
    partial, behind, ahead = lax.optimization_barrier((partial, behind, ahead))
    far = [shift(behind[:middle], "x", 1), shift(ahead[middle:], "x", -1)]
    partial = exchange(partial.reshape(N_HST, query_rows, query_cols), HST)
    query_cos, query_sin = rotary_tables(query_pos)
    own_queries = rotate(jnp.sum(partial.astype(F32), axis=0), query_cos, query_sin).astype(BF16)
    packed = jnp.concatenate([own_queries, own_anchor.reshape(-1, query_cols)], axis=0)
    packed = spread(packed, HST, N_HST)
    all_queries = packed[:, :query_rows].reshape(N_HST * query_rows, query_cols)
    anchors = packed[:, query_rows:].reshape(N_HST, 2, BLK // N_HST, HD)
    anchor_key = anchors[:, 0].reshape(BLK, HD)
    anchor_value = anchors[:, 1].reshape(BLK, HD)

    live = jnp.repeat(cached_mask == 1, BLK)
    bias = jnp.where(live, 0.0, DEAD).astype(F32)[None, :]
    weighted, stats = cached_attention(
        all_queries, cache_keys.reshape(-1, HD), cache_values.reshape(-1, HD), bias
    )

    places = (fresh_ids[:, None] * BLK + jnp.arange(BLK, dtype=jnp.int32)[None, :]).reshape(-1)
    cosine, sine = rotary_tables(places)
    fresh_key, fresh_value = key_value(fresh_states, w_both, cosine, sine)

    weighted, far, pieces = lax.optimization_barrier((weighted, far, pieces))
    pieces = pieces + [shift(piece, "core", 1) for piece in pieces]
    weights = [w_query, ahead, behind] + far
    sums = context_attention(all_queries, fresh_key, fresh_value, weighted, stats)
    spots, sums = lax.optimization_barrier((spots, sums))
    sums = exchange(sums.reshape(N_HST, query_rows, -1), HST)
    context = exchange(combine(sums), HST)
    product = jnp.dot(
        context.reshape(N_HST * query_rows, query_cols), w_output, preferred_element_type=F32
    )
    product = exchange(product.reshape(N_HEAD, -1, product.shape[1]), HEAD)
    query_output = jnp.sum(product, axis=0).astype(BF16)

    products = share_products(spots, fresh_states, pieces, weights)
    queries = lax.psum_scatter(
        products.reshape(-1, query_cols), "z", scatter_dimension=0, tiled=True
    )
    fresh_context = fresh_attention(
        [queries], (cosine, sine, fresh_key, fresh_value, anchor_key, anchor_value)
    )
    return fresh_context, query_output


def solution(mesh):
    mesh = Mesh(mesh.devices.reshape(RING, RING, RING, 2), HST + HEAD)
    return jax.shard_map(
        body,
        mesh=mesh,
        in_specs=(
            P(HST, None),
            P(HST, None),
            P(HST, HEAD),
            P(HST, HEAD),
            P(HST, HEAD),
            P(HEAD, HST),
            P(HST, None, HEAD),
            P(HST, None, HEAD),
            P(HST),
            P(HST),
            P(),
            P(HST),
        ),
        out_specs=(P(HST, HEAD), P(HEAD, HST)),
        check_vma=False,
    )
```

```python
import functools
import math

import jax
import jax.numpy as jnp
from jax import lax
from jax.experimental import pallas as pl
from jax.experimental.pallas import tpu as pltpu
from jax.sharding import Mesh
from jax.sharding import PartitionSpec as P

HD = 128
BLK = 256
FRESH_BLK = 2
ROPE_BASE = 500000.0
N_HST = 16
N_HEAD = 8
RING = 4
STEP_HEADS = 2
HST = ("z", "x")
HEAD = ("y", "core")
SCALE = math.log2(math.e) / math.sqrt(HD)
BF16 = jnp.bfloat16
F32 = jnp.float32
VMEM_LIMIT = 48 * 1024 * 1024
DEAD = -1e30


def scaled_rates(width):
    half = width // 2
    base_rates = ROPE_BASE ** (-jnp.arange(half, dtype=F32) * (2.0 / width))
    wavelength = 2.0 * math.pi / base_rates
    smooth = jnp.clip((8192.0 / wavelength - 1.0) / 3.0, 0.0, 1.0)
    return (1.0 - smooth) * base_rates / 8.0 + smooth * base_rates


def rotary_tables(places):
    angles = places.astype(F32)[:, None] * scaled_rates(HD)[None, :]
    cosine, sine = jnp.cos(angles), jnp.sin(angles)
    return (
        jnp.concatenate([cosine, cosine], axis=1),
        jnp.concatenate([-sine, sine], axis=1),
    )


def rotate(vectors, cosine, sine):
    rows, cols = vectors.shape
    split = vectors.reshape(rows, cols // HD, HD)
    swapped = jnp.concatenate([split[..., HD // 2 :], split[..., : HD // 2]], axis=-1)
    return (split * cosine[:, None, :] + swapped * sine[:, None, :]).reshape(rows, cols)


def dot_t(a, b):
    return lax.dot_general(a, b, (((1,), (1,)), ((), ())), preferred_element_type=F32)


def fresh_kernel(count, *refs):
    parts, refs = refs[:count], refs[count:]
    cos_ref, sin_ref, k_ref, v_ref, ak_ref, av_ref, out_ref = refs
    row = lax.broadcasted_iota(jnp.int32, (BLK, BLK), 0)
    col = lax.broadcasted_iota(jnp.int32, (BLK, BLK), 1)
    causal = col <= row
    for g in range(out_ref.shape[1] // HD):
        cols = slice(g * HD, (g + 1) * HD)
        q = parts[0][:, cols].astype(F32)
        for part in parts[1:]:
            q += part[:, cols].astype(F32)
        q = (q * cos_ref[...] + pltpu.roll(q, HD // 2, 1) * sin_ref[...]).astype(BF16)
        for b in range(FRESH_BLK):
            rows = slice(b * BLK, (b + 1) * BLK)
            qb = q[rows]
            s0 = dot_t(qb, ak_ref[...]) * SCALE
            s1 = jnp.where(causal, dot_t(qb, k_ref[rows, :]) * SCALE, -jnp.inf)
            top = jnp.max(jnp.maximum(s0, s1), axis=1, keepdims=True)
            e0 = jnp.exp2(s0 - top)
            e1 = jnp.exp2(s1 - top)
            total = jnp.sum(e0 + e1, axis=1, keepdims=True)
            mixed = jnp.dot(e0.astype(BF16), av_ref[...], preferred_element_type=F32)
            mixed += jnp.dot(e1.astype(BF16), v_ref[rows, :], preferred_element_type=F32)
            out_ref[rows, cols] = (mixed / total).astype(BF16)


def fresh_attention(parts, rest):
    rows, cols = parts[0].shape
    wide = STEP_HEADS * HD
    whole = lambda a: pl.BlockSpec(a.shape, lambda i: (0, 0))
    return pl.pallas_call(
        functools.partial(fresh_kernel, len(parts)),
        grid=(cols // wide,),
        in_specs=[pl.BlockSpec((rows, wide), lambda i: (0, i))] * len(parts)
        + [whole(a) for a in rest],
        out_specs=pl.BlockSpec((rows, wide), lambda i: (0, i)),
        out_shape=jax.ShapeDtypeStruct((rows, cols), BF16),
        compiler_params=pltpu.CompilerParams(vmem_limit_bytes=VMEM_LIMIT),
        cost_estimate=pl.CostEstimate(
            flops=rows * (cols // HD) * 2 * BLK * HD * 4,
            bytes_accessed=rows * cols * 4,
            transcendentals=rows * (cols // HD) * 2 * BLK,
        ),
        name="fresh_attention",
    )(*parts, *rest)


def shares_kernel(count, place_ref, states_ref, *refs):
    pieces, w_refs = refs[:count], refs[count : count + 5]
    out_ref, t_v, w_v, o_v, t_sem, s_sem, w_sem, o_sem = refs[count + 5 :]
    blocks, rows, depth = t_v.shape
    slab = pieces[0].shape[1]
    own_copy = pltpu.make_async_copy(
        states_ref.at[:, pl.ds(pl.multiple_of(place_ref[0] * depth, depth), depth)],
        t_v.at[0],
        s_sem,
    )
    own_copy.start()
    w_copies = []
    for i, ref in enumerate(w_refs):
        at = pl.multiple_of(place_ref[blocks + count + i], slab)
        copy = pltpu.make_async_copy(ref, w_v.at[pl.ds(at, ref.shape[0]), :], w_sem.at[i])
        copy.start()
        w_copies.append(copy)
    copies = []
    for b in range(blocks - 1):
        for i, piece in enumerate(pieces):
            copy = pltpu.make_async_copy(
                piece.at[pl.ds(b * rows, rows), :],
                t_v.at[b + 1, :, pl.ds(pl.multiple_of(place_ref[blocks + i], slab), slab)],
                t_sem.at[b, i],
            )
            copy.start()
            copies.append(copy)
    own_copy.wait()
    for copy in w_copies:
        copy.wait()
    out_copies = []
    for b in range(blocks):
        if b > 0:
            for copy in copies[(b - 1) * count : b * count]:
                copy.wait()
        for n in range(0, w_v.shape[1], COLS):
            o_v[b, :, n : n + COLS] = jnp.dot(
                t_v[b], w_v[:, n : n + COLS], preferred_element_type=F32
            ).astype(BF16)
        copy = pltpu.make_async_copy(o_v.at[b], out_ref.at[place_ref[b]], o_sem.at[b])
        copy.start()
        out_copies.append(copy)
    for copy in out_copies:
        copy.wait()


def share_products(places, states, pieces, weights):
    blocks = RING
    rows = states.shape[0]
    depth = blocks * weights[0].shape[0]
    cols = weights[0].shape[1]
    anywhere = pl.BlockSpec(memory_space=pl.ANY)
    return pl.pallas_call(
        functools.partial(shares_kernel, len(pieces)),
        grid_spec=pltpu.PrefetchScalarGridSpec(
            num_scalar_prefetch=1,
            grid=(1,),
            in_specs=[anywhere] * (1 + len(pieces) + len(weights)),
            out_specs=anywhere,
            scratch_shapes=[
                pltpu.VMEM((blocks, rows, depth), BF16),
                pltpu.VMEM((depth, cols), BF16),
                pltpu.VMEM((blocks, rows, cols), BF16),
                pltpu.SemaphoreType.DMA((blocks - 1, len(pieces))),
                pltpu.SemaphoreType.DMA,
                pltpu.SemaphoreType.DMA((len(weights),)),
                pltpu.SemaphoreType.DMA((blocks,)),
            ],
        ),
        out_shape=jax.ShapeDtypeStruct((blocks, rows, cols), BF16),
        compiler_params=pltpu.CompilerParams(vmem_limit_bytes=VMEM_LIMIT),
        cost_estimate=pl.CostEstimate(
            flops=blocks * rows * depth * cols * 2,
            bytes_accessed=(blocks * rows * (depth + cols) + depth * cols) * 2,
            transcendentals=0,
        ),
        name="share_products",
    )(places, states, *pieces, *weights)


def key_value_kernel(states_ref, w_ref, cos_ref, sin_ref, k_ref, v_ref, acc_ref):
    step = pl.program_id(0)

    @pl.when(step == 0)
    def _():
        acc_ref[...] = jnp.zeros_like(acc_ref)

    acc_ref[...] += jnp.dot(states_ref[...], w_ref[...], preferred_element_type=F32)

    @pl.when(step == pl.num_programs(0) - 1)
    def _():
        k = acc_ref[:, :HD]
        k = k * cos_ref[...] + pltpu.roll(k, HD // 2, 1) * sin_ref[...]
        k_ref[...] = k.astype(BF16)
        v_ref[...] = acc_ref[:, HD:].astype(BF16)


def key_value(states, weights, cosine, sine):
    rows, depth = states.shape
    step = 2048
    whole = lambda a: pl.BlockSpec(a.shape, lambda i: (0, 0))
    out = jax.ShapeDtypeStruct((rows, HD), BF16)
    return pl.pallas_call(
        key_value_kernel,
        grid=(depth // step,),
        in_specs=[
            pl.BlockSpec((rows, step), lambda i: (0, i)),
            pl.BlockSpec((step, 2 * HD), lambda i: (i, 0)),
            whole(cosine),
            whole(sine),
        ],
        out_specs=[whole(out), whole(out)],
        out_shape=[out, out],
        scratch_shapes=[pltpu.VMEM((rows, 2 * HD), F32)],
        compiler_params=pltpu.CompilerParams(vmem_limit_bytes=VMEM_LIMIT),
        cost_estimate=pl.CostEstimate(
            flops=rows * depth * 4 * HD,
            bytes_accessed=(rows + 2 * HD) * depth * 2,
            transcendentals=0,
        ),
        name="key_value",
    )(states, weights, cosine, sine)


CHUNK = 512
COLS = 512


def pieces_of(value):
    high = value.astype(BF16).astype(F32)
    middle = (value - high).astype(BF16).astype(F32)
    return high, middle, value - high - middle


def cached_kernel(q_ref, k_ref, v_ref, bias_ref, out_ref, stat_ref, s_ref):
    step = pl.program_id(0)
    rows = q_ref.shape[0]
    q = jnp.concatenate([q_ref[:, g * HD : (g + 1) * HD] for g in range(STEP_HEADS)], axis=0)
    places = range(0, k_ref.shape[0], CHUNK)
    top = None
    for at in places:
        s = dot_t(q, k_ref[at : at + CHUNK, :]) * SCALE + bias_ref[:, at : at + CHUNK]
        s_ref[:, at : at + CHUNK] = s
        for j in range(0, CHUNK, HD):
            top = s[:, j : j + HD] if top is None else jnp.maximum(top, s[:, j : j + HD])
    peak = jnp.max(top, axis=1, keepdims=True)
    total = jnp.zeros((q.shape[0], HD), F32)
    acc = jnp.zeros((q.shape[0], HD), F32)
    for at in places:
        e = jnp.exp2(s_ref[:, at : at + CHUNK] - peak)
        for j in range(0, CHUNK, HD):
            total += e[:, j : j + HD]
        acc += jnp.dot(e.astype(BF16), v_ref[at : at + CHUNK, :], preferred_element_type=F32)
    total = jnp.sum(total, axis=1, keepdims=True)

    @pl.when(step == 0)
    def _():
        stat_ref[...] = jnp.zeros_like(stat_ref)

    lane = lax.broadcasted_iota(jnp.int32, (rows, HD), 1)
    stats = stat_ref[...]
    for g in range(STEP_HEADS):
        block = slice(g * rows, (g + 1) * rows)
        for n, number in enumerate((peak, total)):
            place = step * STEP_HEADS + g + n * N_HEAD
            stats = jnp.where(lane == place, number[block], stats)
        out_ref[:, g * HD : (g + 1) * HD] = acc[block]
    stat_ref[...] = stats


def cached_attention(q, key, value, bias):
    rows, cols = q.shape
    wide = STEP_HEADS * HD
    keys = key.shape[0]
    whole = lambda a: pl.BlockSpec(a.shape, lambda i: (0, 0))
    stats = jax.ShapeDtypeStruct((rows, HD), F32)
    return pl.pallas_call(
        cached_kernel,
        grid=(cols // wide,),
        in_specs=[pl.BlockSpec((rows, wide), lambda i: (0, i))]
        + [whole(a) for a in (key, value, bias)],
        out_specs=[pl.BlockSpec((rows, wide), lambda i: (0, i)), whole(stats)],
        out_shape=[jax.ShapeDtypeStruct((rows, cols), F32), stats],
        scratch_shapes=[pltpu.VMEM((STEP_HEADS * rows, keys), F32)],
        compiler_params=pltpu.CompilerParams(vmem_limit_bytes=VMEM_LIMIT),
        cost_estimate=pl.CostEstimate(
            flops=rows * cols * keys * 4,
            bytes_accessed=keys * HD * 4 + rows * cols * 4,
            transcendentals=rows * (cols // HD) * keys,
        ),
        name="cached_attention",
    )(q, key, value, bias)


def context_kernel(q_ref, k_ref, v_ref, old_ref, stat_ref, out_ref):
    rows, cols = q_ref.shape
    heads = cols // HD
    lane = lax.broadcasted_iota(jnp.int32, (rows, HD), 1)
    old_stats = stat_ref[...]
    stats = jnp.zeros((rows, HD), F32)
    for first in range(0, heads, STEP_HEADS):
        group = range(first, first + STEP_HEADS)
        q = jnp.concatenate([q_ref[:, g * HD : (g + 1) * HD] for g in group], axis=0)
        old = jnp.concatenate([old_ref[:, g * HD : (g + 1) * HD] for g in group], axis=0)
        old_peak = jnp.concatenate([old_stats[:, g : g + 1] for g in group], axis=0)
        old_total = jnp.concatenate(
            [old_stats[:, N_HEAD + g : N_HEAD + g + 1] for g in group], axis=0
        )
        s = dot_t(q, k_ref[...]) * SCALE
        peak = jnp.maximum(jnp.max(s, axis=1, keepdims=True), old_peak)
        e = jnp.exp2(s - peak)
        factor = jnp.exp2(old_peak - peak)
        total = jnp.sum(e, axis=1, keepdims=True) + old_total * factor
        acc = jnp.dot(e.astype(BF16), v_ref[...], preferred_element_type=F32) + old * factor
        numbers = pieces_of(peak) + pieces_of(total)
        for i, g in enumerate(group):
            block = slice(i * rows, (i + 1) * rows)
            for n, number in enumerate(numbers):
                stats = jnp.where(lane == g + n * N_HEAD, number[block], stats)
            out_ref[:, g * HD : (g + 1) * HD] = acc[block].astype(BF16)
    out_ref[:, cols:] = stats.astype(BF16)


def context_attention(q, key, value, old, old_stats):
    rows, cols = q.shape
    keys = key.shape[0]
    return pl.pallas_call(
        context_kernel,
        out_shape=jax.ShapeDtypeStruct((rows, cols + HD), BF16),
        compiler_params=pltpu.CompilerParams(vmem_limit_bytes=VMEM_LIMIT),
        cost_estimate=pl.CostEstimate(
            flops=rows * cols * keys * 4,
            bytes_accessed=keys * HD * 4 + rows * cols * 8,
            transcendentals=rows * (cols // HD) * keys,
        ),
        name="context_attention",
    )(q, key, value, old, old_stats)


def combine_kernel(parts_ref, out_ref):
    heads = out_ref.shape[2] // HD
    stats = parts_ref[:, :, heads * HD :].astype(F32)
    stats = (
        stats
        + pltpu.roll(stats, HD - N_HEAD, 2)
        + pltpu.roll(stats, HD - 2 * N_HEAD, 2)
    )
    factors = jnp.exp2(stats - jnp.max(stats, axis=0, keepdims=True))
    totals = pltpu.roll(stats, HD - 3 * N_HEAD, 2)
    share = factors / jnp.sum(totals * factors, axis=0, keepdims=True)
    for g in range(heads):
        cols = slice(g * HD, (g + 1) * HD)
        mixed = jnp.sum(parts_ref[:, :, cols].astype(F32) * share[:, :, g : g + 1], axis=0)
        out_ref[:, :, cols] = jnp.broadcast_to(
            mixed.astype(BF16)[None], out_ref.shape[:2] + (HD,)
        )


def combine(parts):
    groups, rows, cols = parts.shape
    return pl.pallas_call(
        combine_kernel,
        out_shape=jax.ShapeDtypeStruct((groups, rows, cols - HD), BF16),
        compiler_params=pltpu.CompilerParams(vmem_limit_bytes=VMEM_LIMIT),
        name="combine",
    )(parts)


def shift(value, axis, by):
    size = RING if axis != "core" else 2
    return lax.ppermute(value, axis, [(i, (i + by) % size) for i in range(size)])


def exchange(value, axis):
    return lax.all_to_all(value, axis, 0, 0, tiled=True)


def spread(value, axis, count):
    return exchange(jnp.broadcast_to(value[None], (count,) + value.shape), axis)


def body(
    fresh_states,
    query_states,
    w_query,
    w_key,
    w_value,
    w_output,
    cache_keys,
    cache_values,
    cached_mask,
    fresh_ids,
    anchor_id,
    query_pos,
):
    fresh_rows = fresh_states.shape[0]
    query_rows, width = query_states.shape
    depth, query_cols = w_query.shape
    held_blocks = cache_keys.shape[0]

    w_both = lax.all_gather(
        jnp.concatenate([w_key, w_value], axis=1), HST, axis=0, tiled=True
    )

    z, x, y, core = (lax.axis_index(a) for a in ("z", "x", "y", "core"))
    quarter = width // RING
    slab = quarter // N_HEAD
    steps = (1, -1, 2)
    slices = [
        lax.dynamic_slice_in_dim(
            fresh_states,
            lax.rem(z + d + RING, RING) * quarter + (y * 2 + core) * slab,
            slab,
            axis=1,
        )
        for d in steps
    ]
    owners = lax.rem(y + jnp.arange(RING, dtype=jnp.int32), RING) * 2
    at = jnp.concatenate([owners + core, owners + 1 - core]) * slab
    sources = jnp.stack([lax.rem(z - d + RING, RING) for d in steps])
    behind, ahead = shift(w_query, "x", 1), shift(w_query, "x", -1)
    middle = depth // 2
    turn = lax.rem(x + jnp.array([0, 1, 3, 2, 2], jnp.int32), RING) * depth
    turn = turn + jnp.array([0, 0, 0, 0, middle], jnp.int32)
    spots = jnp.concatenate([z[None], sources, at, turn])

    anchor = anchor_id[0]
    holder = lax.axis_index(HST) == anchor // held_blocks
    held = anchor % held_blocks
    anchor_parts = [
        jnp.where(holder, lax.dynamic_index_in_dim(a, held, 0, keepdims=False), 0).reshape(
            N_HST, -1, depth
        )
        for a in (cache_keys, cache_values)
    ]
    states = query_states.reshape(query_rows, N_HST, depth).transpose(1, 0, 2)
    packed = jnp.concatenate([states] + anchor_parts, axis=1)
    packed, slices = lax.optimization_barrier((packed, slices))
    mine = jnp.concatenate([shift(v, "z", d) for v, d in zip(slices, steps)], axis=0)
    got = exchange(packed, HST)
    got, mine = lax.optimization_barrier((got, mine))
    pieces = [mine, shift(mine, "y", -1), shift(mine, "y", 2), shift(mine, "y", 1)]
    own_anchor = jnp.sum(got[:, query_rows:].astype(F32), axis=0).astype(BF16)
    states = got[:, :query_rows].reshape(N_HST * query_rows, depth)

    partial = jnp.dot(states, w_query, preferred_element_type=F32).astype(BF16)
    partial, behind, ahead = lax.optimization_barrier((partial, behind, ahead))
    far = [shift(behind[:middle], "x", 1), shift(ahead[middle:], "x", -1)]
    partial = exchange(partial.reshape(N_HST, query_rows, query_cols), HST)
    query_cos, query_sin = rotary_tables(query_pos)
    own_queries = rotate(jnp.sum(partial.astype(F32), axis=0), query_cos, query_sin).astype(BF16)
    packed = jnp.concatenate([own_queries, own_anchor.reshape(-1, query_cols)], axis=0)
    packed = spread(packed, HST, N_HST)
    all_queries = packed[:, :query_rows].reshape(N_HST * query_rows, query_cols)
    anchors = packed[:, query_rows:].reshape(N_HST, 2, BLK // N_HST, HD)
    anchor_key = anchors[:, 0].reshape(BLK, HD)
    anchor_value = anchors[:, 1].reshape(BLK, HD)

    live = jnp.repeat(cached_mask == 1, BLK)
    bias = jnp.where(live, 0.0, DEAD).astype(F32)[None, :]
    weighted, stats = cached_attention(
        all_queries, cache_keys.reshape(-1, HD), cache_values.reshape(-1, HD), bias
    )

    places = (fresh_ids[:, None] * BLK + jnp.arange(BLK, dtype=jnp.int32)[None, :]).reshape(-1)
    cosine, sine = rotary_tables(places)
    fresh_key, fresh_value = key_value(fresh_states, w_both, cosine, sine)

    weighted, far, pieces, spots = lax.optimization_barrier((weighted, far, pieces, spots))
    pieces = pieces + [shift(piece, "core", 1) for piece in pieces]
    weights = [w_query, ahead, behind] + far
    sums = context_attention(all_queries, fresh_key, fresh_value, weighted, stats)
    sums = exchange(sums.reshape(N_HST, query_rows, -1), HST)
    context = exchange(combine(sums), HST)
    product = jnp.dot(
        context.reshape(N_HST * query_rows, query_cols), w_output, preferred_element_type=F32
    )
    product = exchange(product.reshape(N_HEAD, -1, product.shape[1]), HEAD)
    query_output = jnp.sum(product, axis=0).astype(BF16)

    products = share_products(spots, fresh_states, pieces, weights)
    queries = lax.psum_scatter(
        products.reshape(-1, query_cols), "z", scatter_dimension=0, tiled=True
    )
    fresh_context = fresh_attention(
        [queries], (cosine, sine, fresh_key, fresh_value, anchor_key, anchor_value)
    )
    return fresh_context, query_output


def solution(mesh):
    mesh = Mesh(mesh.devices.reshape(RING, RING, RING, 2), HST + HEAD)
    return jax.shard_map(
        body,
        mesh=mesh,
        in_specs=(
            P(HST, None),
            P(HST, None),
            P(HST, HEAD),
            P(HST, HEAD),
            P(HST, HEAD),
            P(HEAD, HST),
            P(HST, None, HEAD),
            P(HST, None, HEAD),
            P(HST),
            P(HST),
            P(),
            P(HST),
        ),
        out_specs=(P(HST, HEAD), P(HEAD, HST)),
        check_vma=False,
    )
```

```python
import functools
import math

import jax
import jax.numpy as jnp
from jax import lax
from jax.experimental import pallas as pl
from jax.experimental.pallas import tpu as pltpu
from jax.sharding import Mesh
from jax.sharding import PartitionSpec as P

HD = 128
BLK = 256
FRESH_BLK = 2
ROPE_BASE = 500000.0
N_HST = 16
N_HEAD = 8
RING = 4
STEP_HEADS = 2
HST = ("z", "x")
HEAD = ("y", "core")
SCALE = math.log2(math.e) / math.sqrt(HD)
BF16 = jnp.bfloat16
F32 = jnp.float32
VMEM_LIMIT = 48 * 1024 * 1024
DEAD = -1e30


def scaled_rates(width):
    half = width // 2
    base_rates = ROPE_BASE ** (-jnp.arange(half, dtype=F32) * (2.0 / width))
    wavelength = 2.0 * math.pi / base_rates
    smooth = jnp.clip((8192.0 / wavelength - 1.0) / 3.0, 0.0, 1.0)
    return (1.0 - smooth) * base_rates / 8.0 + smooth * base_rates


def rotary_tables(places):
    angles = places.astype(F32)[:, None] * scaled_rates(HD)[None, :]
    cosine, sine = jnp.cos(angles), jnp.sin(angles)
    return (
        jnp.concatenate([cosine, cosine], axis=1),
        jnp.concatenate([-sine, sine], axis=1),
    )


def rotate(vectors, cosine, sine):
    rows, cols = vectors.shape
    split = vectors.reshape(rows, cols // HD, HD)
    swapped = jnp.concatenate([split[..., HD // 2 :], split[..., : HD // 2]], axis=-1)
    return (split * cosine[:, None, :] + swapped * sine[:, None, :]).reshape(rows, cols)


def dot_t(a, b):
    return lax.dot_general(a, b, (((1,), (1,)), ((), ())), preferred_element_type=F32)


def fresh_kernel(count, *refs):
    parts, refs = refs[:count], refs[count:]
    cos_ref, sin_ref, k_ref, v_ref, ak_ref, av_ref, out_ref = refs
    row = lax.broadcasted_iota(jnp.int32, (BLK, BLK), 0)
    col = lax.broadcasted_iota(jnp.int32, (BLK, BLK), 1)
    causal = col <= row
    for g in range(out_ref.shape[1] // HD):
        cols = slice(g * HD, (g + 1) * HD)
        q = parts[0][:, cols].astype(F32)
        for part in parts[1:]:
            q += part[:, cols].astype(F32)
        q = (q * cos_ref[...] + pltpu.roll(q, HD // 2, 1) * sin_ref[...]).astype(BF16)
        for b in range(FRESH_BLK):
            rows = slice(b * BLK, (b + 1) * BLK)
            qb = q[rows]
            s0 = dot_t(qb, ak_ref[...]) * SCALE
            s1 = jnp.where(causal, dot_t(qb, k_ref[rows, :]) * SCALE, -jnp.inf)
            top = jnp.max(jnp.maximum(s0, s1), axis=1, keepdims=True)
            e0 = jnp.exp2(s0 - top)
            e1 = jnp.exp2(s1 - top)
            total = jnp.sum(e0 + e1, axis=1, keepdims=True)
            mixed = jnp.dot(e0.astype(BF16), av_ref[...], preferred_element_type=F32)
            mixed += jnp.dot(e1.astype(BF16), v_ref[rows, :], preferred_element_type=F32)
            out_ref[rows, cols] = (mixed / total).astype(BF16)


def fresh_attention(parts, rest):
    rows, cols = parts[0].shape
    wide = STEP_HEADS * HD
    whole = lambda a: pl.BlockSpec(a.shape, lambda i: (0, 0))
    return pl.pallas_call(
        functools.partial(fresh_kernel, len(parts)),
        grid=(cols // wide,),
        in_specs=[pl.BlockSpec((rows, wide), lambda i: (0, i))] * len(parts)
        + [whole(a) for a in rest],
        out_specs=pl.BlockSpec((rows, wide), lambda i: (0, i)),
        out_shape=jax.ShapeDtypeStruct((rows, cols), BF16),
        compiler_params=pltpu.CompilerParams(vmem_limit_bytes=VMEM_LIMIT),
        cost_estimate=pl.CostEstimate(
            flops=rows * (cols // HD) * 2 * BLK * HD * 4,
            bytes_accessed=rows * cols * 4,
            transcendentals=rows * (cols // HD) * 2 * BLK,
        ),
        name="fresh_attention",
    )(*parts, *rest)


def shares_kernel(count, place_ref, states_ref, *refs):
    pieces, w_refs = refs[:count], refs[count : count + 5]
    out_ref, t_v, w_v, o_v, t_sem, s_sem, w_sem, o_sem = refs[count + 5 :]
    blocks, rows, depth = t_v.shape
    slab = pieces[0].shape[1]
    own_copy = pltpu.make_async_copy(
        states_ref.at[:, pl.ds(pl.multiple_of(place_ref[0] * depth, depth), depth)],
        t_v.at[0],
        s_sem,
    )
    own_copy.start()
    w_copies = []
    for i, ref in enumerate(w_refs):
        at = pl.multiple_of(place_ref[blocks + count + i], slab)
        copy = pltpu.make_async_copy(ref, w_v.at[pl.ds(at, ref.shape[0]), :], w_sem.at[i])
        copy.start()
        w_copies.append(copy)
    copies = []
    for b in range(blocks - 1):
        for i, piece in enumerate(pieces):
            copy = pltpu.make_async_copy(
                piece.at[pl.ds(b * rows, rows), :],
                t_v.at[b + 1, :, pl.ds(pl.multiple_of(place_ref[blocks + i], slab), slab)],
                t_sem.at[b, i],
            )
            copy.start()
            copies.append(copy)
    own_copy.wait()
    for copy in w_copies:
        copy.wait()
    out_copies = []
    for b in range(blocks):
        if b > 0:
            for copy in copies[(b - 1) * count : b * count]:
                copy.wait()
        for i, n in enumerate(range(0, w_v.shape[1], COLS)):
            o_v[b, :, n : n + COLS] = jnp.dot(
                t_v[b], w_v[:, n : n + COLS], preferred_element_type=F32
            ).astype(BF16)
            copy = pltpu.make_async_copy(
                o_v.at[b, :, pl.ds(n, COLS)],
                out_ref.at[place_ref[b], :, pl.ds(n, COLS)],
                o_sem.at[b, i],
            )
            copy.start()
            out_copies.append(copy)
    for copy in out_copies:
        copy.wait()


def share_products(places, states, pieces, weights):
    blocks = RING
    rows = states.shape[0]
    depth = blocks * weights[0].shape[0]
    cols = weights[0].shape[1]
    anywhere = pl.BlockSpec(memory_space=pl.ANY)
    return pl.pallas_call(
        functools.partial(shares_kernel, len(pieces)),
        grid_spec=pltpu.PrefetchScalarGridSpec(
            num_scalar_prefetch=1,
            grid=(1,),
            in_specs=[anywhere] * (1 + len(pieces) + len(weights)),
            out_specs=anywhere,
            scratch_shapes=[
                pltpu.VMEM((blocks, rows, depth), BF16),
                pltpu.VMEM((depth, cols), BF16),
                pltpu.VMEM((blocks, rows, cols), BF16),
                pltpu.SemaphoreType.DMA((blocks - 1, len(pieces))),
                pltpu.SemaphoreType.DMA,
                pltpu.SemaphoreType.DMA((len(weights),)),
                pltpu.SemaphoreType.DMA((blocks, cols // COLS)),
            ],
        ),
        out_shape=jax.ShapeDtypeStruct((blocks, rows, cols), BF16),
        compiler_params=pltpu.CompilerParams(vmem_limit_bytes=VMEM_LIMIT),
        cost_estimate=pl.CostEstimate(
            flops=blocks * rows * depth * cols * 2,
            bytes_accessed=(blocks * rows * (depth + cols) + depth * cols) * 2,
            transcendentals=0,
        ),
        name="share_products",
    )(places, states, *pieces, *weights)


def key_value_kernel(states_ref, w_ref, cos_ref, sin_ref, k_ref, v_ref, acc_ref):
    step = pl.program_id(0)

    @pl.when(step == 0)
    def _():
        acc_ref[...] = jnp.zeros_like(acc_ref)

    acc_ref[...] += jnp.dot(states_ref[...], w_ref[...], preferred_element_type=F32)

    @pl.when(step == pl.num_programs(0) - 1)
    def _():
        k = acc_ref[:, :HD]
        k = k * cos_ref[...] + pltpu.roll(k, HD // 2, 1) * sin_ref[...]
        k_ref[...] = k.astype(BF16)
        v_ref[...] = acc_ref[:, HD:].astype(BF16)


def key_value(states, weights, cosine, sine):
    rows, depth = states.shape
    step = 2048
    whole = lambda a: pl.BlockSpec(a.shape, lambda i: (0, 0))
    out = jax.ShapeDtypeStruct((rows, HD), BF16)
    return pl.pallas_call(
        key_value_kernel,
        grid=(depth // step,),
        in_specs=[
            pl.BlockSpec((rows, step), lambda i: (0, i)),
            pl.BlockSpec((step, 2 * HD), lambda i: (i, 0)),
            whole(cosine),
            whole(sine),
        ],
        out_specs=[whole(out), whole(out)],
        out_shape=[out, out],
        scratch_shapes=[pltpu.VMEM((rows, 2 * HD), F32)],
        compiler_params=pltpu.CompilerParams(vmem_limit_bytes=VMEM_LIMIT),
        cost_estimate=pl.CostEstimate(
            flops=rows * depth * 4 * HD,
            bytes_accessed=(rows + 2 * HD) * depth * 2,
            transcendentals=0,
        ),
        name="key_value",
    )(states, weights, cosine, sine)


CHUNK = 512
COLS = 512


def pieces_of(value):
    high = value.astype(BF16).astype(F32)
    middle = (value - high).astype(BF16).astype(F32)
    return high, middle, value - high - middle


def cached_kernel(q_ref, k_ref, v_ref, bias_ref, out_ref, stat_ref, s_ref):
    step = pl.program_id(0)
    rows = q_ref.shape[0]
    q = jnp.concatenate([q_ref[:, g * HD : (g + 1) * HD] for g in range(STEP_HEADS)], axis=0)
    places = range(0, k_ref.shape[0], CHUNK)
    top = None
    for at in places:
        s = dot_t(q, k_ref[at : at + CHUNK, :]) * SCALE + bias_ref[:, at : at + CHUNK]
        s_ref[:, at : at + CHUNK] = s
        for j in range(0, CHUNK, HD):
            top = s[:, j : j + HD] if top is None else jnp.maximum(top, s[:, j : j + HD])
    peak = jnp.max(top, axis=1, keepdims=True)
    total = jnp.zeros((q.shape[0], HD), F32)
    acc = jnp.zeros((q.shape[0], HD), F32)
    for at in places:
        e = jnp.exp2(s_ref[:, at : at + CHUNK] - peak)
        for j in range(0, CHUNK, HD):
            total += e[:, j : j + HD]
        acc += jnp.dot(e.astype(BF16), v_ref[at : at + CHUNK, :], preferred_element_type=F32)
    total = jnp.sum(total, axis=1, keepdims=True)

    @pl.when(step == 0)
    def _():
        stat_ref[...] = jnp.zeros_like(stat_ref)

    lane = lax.broadcasted_iota(jnp.int32, (rows, HD), 1)
    stats = stat_ref[...]
    for g in range(STEP_HEADS):
        block = slice(g * rows, (g + 1) * rows)
        for n, number in enumerate((peak, total)):
            place = step * STEP_HEADS + g + n * N_HEAD
            stats = jnp.where(lane == place, number[block], stats)
        out_ref[:, g * HD : (g + 1) * HD] = acc[block]
    stat_ref[...] = stats


def cached_attention(q, key, value, bias):
    rows, cols = q.shape
    wide = STEP_HEADS * HD
    keys = key.shape[0]
    whole = lambda a: pl.BlockSpec(a.shape, lambda i: (0, 0))
    stats = jax.ShapeDtypeStruct((rows, HD), F32)
    return pl.pallas_call(
        cached_kernel,
        grid=(cols // wide,),
        in_specs=[pl.BlockSpec((rows, wide), lambda i: (0, i))]
        + [whole(a) for a in (key, value, bias)],
        out_specs=[pl.BlockSpec((rows, wide), lambda i: (0, i)), whole(stats)],
        out_shape=[jax.ShapeDtypeStruct((rows, cols), F32), stats],
        scratch_shapes=[pltpu.VMEM((STEP_HEADS * rows, keys), F32)],
        compiler_params=pltpu.CompilerParams(vmem_limit_bytes=VMEM_LIMIT),
        cost_estimate=pl.CostEstimate(
            flops=rows * cols * keys * 4,
            bytes_accessed=keys * HD * 4 + rows * cols * 4,
            transcendentals=rows * (cols // HD) * keys,
        ),
        name="cached_attention",
    )(q, key, value, bias)


def context_kernel(q_ref, k_ref, v_ref, old_ref, stat_ref, out_ref):
    rows, cols = q_ref.shape
    heads = cols // HD
    lane = lax.broadcasted_iota(jnp.int32, (rows, HD), 1)
    old_stats = stat_ref[...]
    stats = jnp.zeros((rows, HD), F32)
    for first in range(0, heads, STEP_HEADS):
        group = range(first, first + STEP_HEADS)
        q = jnp.concatenate([q_ref[:, g * HD : (g + 1) * HD] for g in group], axis=0)
        old = jnp.concatenate([old_ref[:, g * HD : (g + 1) * HD] for g in group], axis=0)
        old_peak = jnp.concatenate([old_stats[:, g : g + 1] for g in group], axis=0)
        old_total = jnp.concatenate(
            [old_stats[:, N_HEAD + g : N_HEAD + g + 1] for g in group], axis=0
        )
        s = dot_t(q, k_ref[...]) * SCALE
        peak = jnp.maximum(jnp.max(s, axis=1, keepdims=True), old_peak)
        e = jnp.exp2(s - peak)
        factor = jnp.exp2(old_peak - peak)
        total = jnp.sum(e, axis=1, keepdims=True) + old_total * factor
        acc = jnp.dot(e.astype(BF16), v_ref[...], preferred_element_type=F32) + old * factor
        numbers = pieces_of(peak) + pieces_of(total)
        for i, g in enumerate(group):
            block = slice(i * rows, (i + 1) * rows)
            for n, number in enumerate(numbers):
                stats = jnp.where(lane == g + n * N_HEAD, number[block], stats)
            out_ref[:, g * HD : (g + 1) * HD] = acc[block].astype(BF16)
    out_ref[:, cols:] = stats.astype(BF16)


def context_attention(q, key, value, old, old_stats):
    rows, cols = q.shape
    keys = key.shape[0]
    return pl.pallas_call(
        context_kernel,
        out_shape=jax.ShapeDtypeStruct((rows, cols + HD), BF16),
        compiler_params=pltpu.CompilerParams(vmem_limit_bytes=VMEM_LIMIT),
        cost_estimate=pl.CostEstimate(
            flops=rows * cols * keys * 4,
            bytes_accessed=keys * HD * 4 + rows * cols * 8,
            transcendentals=rows * (cols // HD) * keys,
        ),
        name="context_attention",
    )(q, key, value, old, old_stats)


def combine_kernel(parts_ref, out_ref):
    heads = out_ref.shape[2] // HD
    stats = parts_ref[:, :, heads * HD :].astype(F32)
    stats = (
        stats
        + pltpu.roll(stats, HD - N_HEAD, 2)
        + pltpu.roll(stats, HD - 2 * N_HEAD, 2)
    )
    factors = jnp.exp2(stats - jnp.max(stats, axis=0, keepdims=True))
    totals = pltpu.roll(stats, HD - 3 * N_HEAD, 2)
    share = factors / jnp.sum(totals * factors, axis=0, keepdims=True)
    for g in range(heads):
        cols = slice(g * HD, (g + 1) * HD)
        mixed = jnp.sum(parts_ref[:, :, cols].astype(F32) * share[:, :, g : g + 1], axis=0)
        out_ref[:, :, cols] = jnp.broadcast_to(
            mixed.astype(BF16)[None], out_ref.shape[:2] + (HD,)
        )


def combine(parts):
    groups, rows, cols = parts.shape
    return pl.pallas_call(
        combine_kernel,
        out_shape=jax.ShapeDtypeStruct((groups, rows, cols - HD), BF16),
        compiler_params=pltpu.CompilerParams(vmem_limit_bytes=VMEM_LIMIT),
        name="combine",
    )(parts)


def shift(value, axis, by):
    size = RING if axis != "core" else 2
    return lax.ppermute(value, axis, [(i, (i + by) % size) for i in range(size)])


def exchange(value, axis):
    return lax.all_to_all(value, axis, 0, 0, tiled=True)


def spread(value, axis, count):
    return exchange(jnp.broadcast_to(value[None], (count,) + value.shape), axis)


def body(
    fresh_states,
    query_states,
    w_query,
    w_key,
    w_value,
    w_output,
    cache_keys,
    cache_values,
    cached_mask,
    fresh_ids,
    anchor_id,
    query_pos,
):
    fresh_rows = fresh_states.shape[0]
    query_rows, width = query_states.shape
    depth, query_cols = w_query.shape
    held_blocks = cache_keys.shape[0]

    w_both = lax.all_gather(
        jnp.concatenate([w_key, w_value], axis=1), HST, axis=0, tiled=True
    )

    z, x, y, core = (lax.axis_index(a) for a in ("z", "x", "y", "core"))
    quarter = width // RING
    slab = quarter // N_HEAD
    steps = (1, -1, 2)
    slices = [
        lax.dynamic_slice_in_dim(
            fresh_states,
            lax.rem(z + d + RING, RING) * quarter + (y * 2 + core) * slab,
            slab,
            axis=1,
        )
        for d in steps
    ]
    owners = lax.rem(y + jnp.arange(RING, dtype=jnp.int32), RING) * 2
    at = jnp.concatenate([owners + core, owners + 1 - core]) * slab
    sources = jnp.stack([lax.rem(z - d + RING, RING) for d in steps])
    behind, ahead = shift(w_query, "x", 1), shift(w_query, "x", -1)
    middle = depth // 2
    turn = lax.rem(x + jnp.array([0, 1, 3, 2, 2], jnp.int32), RING) * depth
    turn = turn + jnp.array([0, 0, 0, 0, middle], jnp.int32)
    spots = jnp.concatenate([z[None], sources, at, turn])

    anchor = anchor_id[0]
    holder = lax.axis_index(HST) == anchor // held_blocks
    held = anchor % held_blocks
    anchor_parts = [
        jnp.where(holder, lax.dynamic_index_in_dim(a, held, 0, keepdims=False), 0).reshape(
            N_HST, -1, depth
        )
        for a in (cache_keys, cache_values)
    ]
    states = query_states.reshape(query_rows, N_HST, depth).transpose(1, 0, 2)
    packed = jnp.concatenate([states] + anchor_parts, axis=1)
    packed, slices = lax.optimization_barrier((packed, slices))
    mine = jnp.concatenate([shift(v, "z", d) for v, d in zip(slices, steps)], axis=0)
    got = exchange(packed, HST)
    got, mine = lax.optimization_barrier((got, mine))
    pieces = [mine, shift(mine, "y", -1), shift(mine, "y", 2), shift(mine, "y", 1)]
    own_anchor = jnp.sum(got[:, query_rows:].astype(F32), axis=0).astype(BF16)
    states = got[:, :query_rows].reshape(N_HST * query_rows, depth)

    partial = jnp.dot(states, w_query, preferred_element_type=F32).astype(BF16)
    partial, behind, ahead = lax.optimization_barrier((partial, behind, ahead))
    far = [shift(behind[:middle], "x", 1), shift(ahead[middle:], "x", -1)]
    partial = exchange(partial.reshape(N_HST, query_rows, query_cols), HST)
    query_cos, query_sin = rotary_tables(query_pos)
    own_queries = rotate(jnp.sum(partial.astype(F32), axis=0), query_cos, query_sin).astype(BF16)
    packed = jnp.concatenate([own_queries, own_anchor.reshape(-1, query_cols)], axis=0)
    packed = spread(packed, HST, N_HST)
    all_queries = packed[:, :query_rows].reshape(N_HST * query_rows, query_cols)
    anchors = packed[:, query_rows:].reshape(N_HST, 2, BLK // N_HST, HD)
    anchor_key = anchors[:, 0].reshape(BLK, HD)
    anchor_value = anchors[:, 1].reshape(BLK, HD)

    live = jnp.repeat(cached_mask == 1, BLK)
    bias = jnp.where(live, 0.0, DEAD).astype(F32)[None, :]
    weighted, stats = cached_attention(
        all_queries, cache_keys.reshape(-1, HD), cache_values.reshape(-1, HD), bias
    )

    places = (fresh_ids[:, None] * BLK + jnp.arange(BLK, dtype=jnp.int32)[None, :]).reshape(-1)
    cosine, sine = rotary_tables(places)
    fresh_key, fresh_value = key_value(fresh_states, w_both, cosine, sine)

    weighted, far, pieces, spots = lax.optimization_barrier((weighted, far, pieces, spots))
    pieces = pieces + [shift(piece, "core", 1) for piece in pieces]
    weights = [w_query, ahead, behind] + far
    sums = context_attention(all_queries, fresh_key, fresh_value, weighted, stats)
    sums = exchange(sums.reshape(N_HST, query_rows, -1), HST)
    context = exchange(combine(sums), HST)
    product = jnp.dot(
        context.reshape(N_HST * query_rows, query_cols), w_output, preferred_element_type=F32
    ).astype(BF16)
    product = exchange(product.reshape(N_HEAD, -1, product.shape[1]), HEAD)
    query_output = jnp.sum(product.astype(F32), axis=0).astype(BF16)

    products = share_products(spots, fresh_states, pieces, weights)
    queries = lax.psum_scatter(
        products.reshape(-1, query_cols), "z", scatter_dimension=0, tiled=True
    )
    fresh_context = fresh_attention(
        [queries], (cosine, sine, fresh_key, fresh_value, anchor_key, anchor_value)
    )
    return fresh_context, query_output


def solution(mesh):
    mesh = Mesh(mesh.devices.reshape(RING, RING, RING, 2), HST + HEAD)
    return jax.shard_map(
        body,
        mesh=mesh,
        in_specs=(
            P(HST, None),
            P(HST, None),
            P(HST, HEAD),
            P(HST, HEAD),
            P(HST, HEAD),
            P(HEAD, HST),
            P(HST, None, HEAD),
            P(HST, None, HEAD),
            P(HST),
            P(HST),
            P(),
            P(HST),
        ),
        out_specs=(P(HST, HEAD), P(HEAD, HST)),
        check_vma=False,
    )
```
